32 devices in a mesh: dp: 16 (over z, y, core), tensor: 2 (over x).
Axes of the slice: x: 2, y: 2, z: 4, core: 2. Of those that a mesh axis runs over, the one named last changes fastest.
Arguments:
- tokens: bfloat16 [8976, 1024], P('dp'), may hold values from -6 to 6
- qkv_weight: bfloat16 [1024, 3, 1024], P(None, None, 'tensor'), may hold values from -0.1875 to 0.1875
- qv_bias: bfloat16 [2, 1024], P(None, 'tensor'), may hold values from -3 to 3
- out_weight: bfloat16 [1024, 1024], P('tensor'), may hold values from -1.5 to 1.5
- out_bias: bfloat16 [1024], replicated, may hold values from -2 to 2
- up_weight: bfloat16 [1024, 4096], P(None, 'tensor'), may hold values from -0.1875 to 0.1875
- up_bias: bfloat16 [4096], P('tensor'), may hold values from -3 to 3
- down_weight: bfloat16 [4096, 1024], P('tensor'), may hold values from -0.09375 to 0.09375
- down_bias: bfloat16 [1024], replicated, may hold values from -2 to 2
- norm_gain: bfloat16 [2, 1024], replicated, may hold values from 0.5 to 1.5
- norm_shift: bfloat16 [2, 1024], replicated, may hold values from -2 to 2
- rel_tables: bfloat16 [3, 128, 16], P(None, None, 'tensor'), may hold values from -5 to 5
- buckets: int32 [16, 3, 561, 561], P('dp'), may hold values from 0 to 127, as said below
- key_mask: int32 [16, 561], P('dp'), may hold values from 0 to 1, as said below
- cotangent: bfloat16 [8976, 1024], P('dp', 'tensor'), may hold values from -6 to 6
Outputs:
- layer_out: bfloat16 [8976, 1024], P('dp', 'tensor')
- grad_tokens: bfloat16 [8976, 1024], P('dp', 'tensor')
- grad_qkv_weight: float32 [1024, 3, 1024], P(None, None, 'tensor')
- grad_qv_bias: float32 [2, 1024], P(None, 'tensor')
- grad_out_weight: float32 [1024, 1024], P('tensor')
- grad_out_bias: float32 [1024], P('tensor')
- grad_up_weight: float32 [1024, 4096], P(None, 'tensor')
- grad_up_bias: float32 [4096], P('tensor')
- grad_down_weight: float32 [4096, 1024], P('tensor')
- grad_down_bias: float32 [1024], P('tensor')
- grad_norm_gain: float32 [2, 1024], P(None, 'tensor')
- grad_norm_shift: float32 [2, 1024], P(None, 'tensor')
- grad_rel_tables: float32 [3, 128, 16], P(None, None, 'tensor')
The draws below stay inside these ranges and needn't reach their ends.
Inputs may be any that keep to these rules, and one draw needn't show every extreme that they name: buckets[page, t, i, j] is the bucket of kind t (1-D, x, y) of the pair (i, j) of the page's positions. `key_mask`: in each page the attended text positions are a leading run of the 512 text slots, of varying length, and all 49 patch positions are attended.
All inputs are finite; a program needn't handle non-finite values.
Results may differ from the reference program's by a relative error of at most 0.02.
Values may be sent and summed in bfloat16 or wider, within the bound.
No kernel may reach another device: no remote copies, remote signals or barrier semaphores. Data moves between devices by JAX's collectives and lax.ppermute only.
A program may use at most 512 MiB of HBM per device.

```python
from functools import partial
import jax
import jax.numpy as jnp
from jax import lax

D = 1024
HEADS = 16
HEAD_DIM = 64
FF = 4096
BUCKETS = 128
TEXT = 512
PATCHES = 49
SEQ = 561
PAGES = 16
TOKENS = 8976


def draw_buckets(key, part):
    coord_key = jax.random.fold_in(key, 11)
    text_coords = jax.random.randint(coord_key, (PAGES, TEXT, 2), 0, 1024)
    text_coords = text_coords.at[:, 0, :].set(0)
    patch_index = jnp.arange(PATCHES, dtype=jnp.int32)
    patch_coords = jnp.stack([patch_index % 7 * 146 + 73, patch_index // 7 * 146 + 73], axis=-1)
    coords = jnp.concatenate([text_coords, jnp.broadcast_to(patch_coords[None], (PAGES, PATCHES, 2))], axis=1)
    advance_key = jax.random.fold_in(key, 37)
    advances = jax.random.randint(advance_key, (PAGES, TEXT), 1, 3)
    text_places = jnp.cumsum(advances, axis=1) - advances[:, :1]
    patch_places = text_places[:, -1:] + 1 + patch_index[None, :]
    places = jnp.concatenate([text_places, patch_places], axis=1).astype(jnp.int32)
    half_range = BUCKETS // 2
    linear = jnp.clip(places[:, :, None] - places[:, None, :], -half_range, half_range - 1) + half_range
    across = jnp.clip(jnp.floor_divide(coords[:, :, None, 0] - coords[:, None, :, 0], 8), -half_range, half_range - 1) + half_range
    vertical = jnp.clip(jnp.floor_divide(coords[:, :, None, 1] - coords[:, None, :, 1], 8), -half_range, half_range - 1) + half_range
    return jnp.stack([linear, across, vertical], axis=1).astype(jnp.int32)


def draw_key_mask(key, part):
    length_key = jax.random.fold_in(key, 23)
    text_length = jax.random.randint(length_key, (PAGES, 1), TEXT // 4, TEXT + 1)
    position = jnp.arange(SEQ, dtype=jnp.int32)[None, :]
    return ((position < text_length) | (position >= TEXT)).astype(jnp.int32)


def steps_of(key, extent, pieces, low, high):
    loudness, own = 1.0, jax.random.fold_in(key, 6)
    for axis_at, parts in pieces:
        draws = jnp.exp(jax.random.uniform(jax.random.fold_in(own, axis_at), (parts,), jnp.float32, low / len(pieces), high / len(pieces)))
        loudness = loudness * jnp.repeat(draws, extent[axis_at] // parts).reshape([-1 if axis == axis_at else 1 for axis in range(len(extent))])
    return loudness


def noise(rng, shape, scale, reach, shards=(), held_as=jnp.bfloat16):
    entries = scale * jax.random.normal(rng, shape, jnp.float32)
    if shards:
        entries = entries * steps_of(rng, shape, shards, -0.22, 0.18)
    return jnp.clip(entries, -reach, reach).astype(held_as)


def setup_inputs(seed: int = 0) -> dict:
    splits = jax.random.split(jax.random.key(seed), 16)
    return {
        "tokens": noise(splits[0], (TOKENS, D), 1.0, 6.0, ((0, 16),)),
        "qkv_weight": noise(splits[1], (D, 3, D), D ** -0.5, 0.1875, ((2, 2),)),
        "qv_bias": noise(splits[2], (2, D), 0.5, 3.0, ((1, 2),)),
        "out_weight": noise(splits[3], (D, D), (D // 64) ** -0.5, 1.5, ((0, 2),)),
        "out_bias": noise(splits[4], (D,), 0.3, 2.0),
        "up_weight": noise(splits[5], (D, FF), D ** -0.5, 0.1875, ((1, 2),)),
        "up_bias": noise(splits[6], (FF,), 0.5, 3.0, ((0, 2),)),
        "down_weight": noise(splits[7], (FF, D), FF ** -0.5, 0.09375, ((0, 2),)),
        "down_bias": noise(splits[8], (D,), 0.3, 2.0),
        "norm_gain": jnp.clip(1.0 + 0.1 * jax.random.normal(splits[9], (2, D), jnp.float32), 0.5, 1.5).astype(jnp.bfloat16),
        "norm_shift": noise(splits[10], (2, D), 0.3, 2.0),
        "rel_tables": noise(splits[11], (3, BUCKETS, HEADS), 1.0, 5.0, ((2, 2),)),
        "buckets": draw_buckets(jax.random.fold_in(splits[15], 71), 0),
        "key_mask": draw_key_mask(jax.random.fold_in(splits[15], 71), 0),
        "cotangent": noise(splits[14], (TOKENS, D), 1.0, 6.0, ((0, 16), (1, 2))),
    }


norm_epsilon = 1e-05
masked_score = -1e+30

@jax.custom_vjp
def low(v):
    return lax.optimization_barrier(v.astype(jnp.bfloat16)).astype(jnp.float32)

@jax.custom_vjp
def low_back(v):
    return v

def low_keep(v):
    return (low(v), None)

def low_pass(kept, grad):
    return (grad,)

def back_keep(v):
    return (v, None)

def back_low(kept, grad):
    return (low(grad),)
low.defvjp(low_keep, low_pass)
low_back.defvjp(back_keep, back_low)

def decode_codes(pair_codes, levels):
    return (pair_codes[0], pair_codes[1], pair_codes[2])

def layer_norm(values, gain, shift):
    center = lax.optimization_barrier(jnp.mean(values, axis=-1, keepdims=True))
    deviation = values - center
    spread = lax.optimization_barrier(jnp.mean(deviation * deviation, axis=-1, keepdims=True))
    return deviation * lax.rsqrt(spread + norm_epsilon) * gain + shift

def page_attention(page_inputs, tables):
    queries, keys_page, values_page, pair_codes, key_valid = page_inputs
    levels = tables.shape[1]
    first_bucket, second_bucket, third_bucket = decode_codes(pair_codes, levels)
    bias = tables[0][first_bucket] + tables[1][second_bucket] + tables[2][third_bucket]
    products = jnp.einsum('qhd,khd->hqk', queries, keys_page, precision=lax.Precision.HIGHEST)
    scores = low_back(products * HEAD_DIM ** (-0.5) + jnp.transpose(bias, (2, 0, 1)))
    scores = jnp.where(key_valid[None, None, :] > 0, scores, masked_score)
    probs = jax.nn.softmax(scores, axis=-1)
    return jnp.einsum('hqk,khd->qhd', low(probs), values_page, precision=lax.Precision.HIGHEST)

def reference(tokens, qkv_weight, qv_bias, out_weight, out_bias, up_weight, up_bias, down_weight, down_bias, norm_gain, norm_shift, rel_tables, buckets, key_mask, cotangent):
    highest = lax.Precision.HIGHEST

    def page_shape(matrix):
        return matrix.reshape(PAGES, SEQ, HEADS, HEAD_DIM)

    def forward(token_rows, qkv_matrix, qv_shift, out_matrix, out_shift, up_matrix, up_shift, down_matrix, down_shift, gain_rows, shifts, tables):
        queries = low(low_back(jnp.dot(token_rows, qkv_matrix[:, 0], precision=highest) + qv_shift[0]))
        keys_all = low(low_back(jnp.dot(token_rows, qkv_matrix[:, 1], precision=highest)))
        values_all = low(low_back(jnp.dot(token_rows, qkv_matrix[:, 2], precision=highest) + qv_shift[1]))
        mixed = lax.map(jax.checkpoint(partial(page_attention, tables=tables)), (page_shape(queries), page_shape(keys_all), page_shape(values_all), buckets, key_mask))
        mixed = low(low_back(mixed.reshape(TOKENS, D)))
        attended = low_back(jnp.dot(mixed, out_matrix, precision=highest) + out_shift)
        normed = layer_norm(token_rows + attended, gain_rows[0], shifts[0])
        pre_act = low_back(jnp.dot(low(normed), up_matrix, precision=highest) + up_shift)
        hidden = low(jax.nn.gelu(pre_act, approximate=False))
        ffn_out = low_back(jnp.dot(hidden, down_matrix, precision=highest) + down_shift)
        return layer_norm(normed + ffn_out, gain_rows[1], shifts[1])
    single = jnp.float32
    outputs, pullback = jax.vjp(forward, tokens.astype(single), qkv_weight.astype(single), qv_bias.astype(single), out_weight.astype(single), out_bias.astype(single), up_weight.astype(single), up_bias.astype(single), down_weight.astype(single), down_bias.astype(single), norm_gain.astype(single), norm_shift.astype(single), rel_tables.astype(single))
    gradients = pullback(cotangent.astype(single))
    return (outputs.astype(jnp.bfloat16), gradients[0].astype(jnp.bfloat16), gradients[1], gradients[2], gradients[3], gradients[4], gradients[5], gradients[6], gradients[7], gradients[8], gradients[9], gradients[10], gradients[11])
```

```python
from functools import partial

import jax
import jax.numpy as jnp
from jax import lax
from jax.experimental import pallas as pl
from jax.experimental.pallas import tpu as pltpu
from jax.sharding import PartitionSpec as P

HEAD_DIM = 64


norm_epsilon = 1e-05
masked_score = -1e30


def exact_gelu(values):
    return jax.nn.gelu(values, approximate=False)


LANES = 128
STEP = 2048.0
RC = 576
RB = 96


def fwd_kernel(length, q_ref, k_ref, v_ref, b_ref, m_ref, t_ref, mixed_ref, p_ref, kz, vz, qz, tail, s_sc):
    pair=pl.program_id(0)
    span=kz.shape[1]
    tall=qz.shape[0]
    full=length//LANES
    rest=length-full*LANES
    @pl.when(pair==0)
    def _():
        kz[...]=jnp.zeros_like(kz)
        vz[...]=jnp.zeros_like(vz)
        qz[...]=jnp.zeros_like(qz)
        tail[...]=jnp.zeros_like(tail)
        for t in range(3):
            tail[t,:length,:rest]=b_ref[0,t,:,full*LANES:]
    low=lax.broadcasted_iota(jnp.int32,(length,LANES),1)<HEAD_DIM
    kk=k_ref[...].astype(jnp.float32)*(HEAD_DIM**-0.5*STEP)
    vv=v_ref[...].astype(jnp.float32)
    kz[0,:length,:]=jnp.where(low,kk,0.0).astype(jnp.bfloat16)
    kz[1,:length,:]=jnp.where(low,0.0,kk).astype(jnp.bfloat16)
    vz[0,:length,:]=jnp.where(low,vv,0.0).astype(jnp.bfloat16)
    vz[1,:length,:]=jnp.where(low,0.0,vv).astype(jnp.bfloat16)
    qz[:length,:]=q_ref[...]
    valid=m_ref[...]>0
    for half in range(2):
        s_sc[half]=lax.dot_general(qz[...],kz[half],(((1,),(1,)),((),())),preferred_element_type=jnp.float32)
    for r in range(0,tall,RC):
        rc=min(RC,tall-r)
        bc=min(rc,length-r)
        tabs=[jnp.broadcast_to(t_ref[0,t:t+1,:],(bc,LANES)) for t in range(3)]
        parts=[[],[]]
        for c in range(span//LANES):
            code=None
            for t in range(3):
                idx=(b_ref[0,t,r:r+bc,c*LANES:(c+1)*LANES] if c<full else tail[t,r:r+bc,:])
                g=jnp.take_along_axis(tabs[t],idx,axis=1,mode="promise_in_bounds")
                code=g if code is None else code+g
            for half in range(2):
                bias=(code>>16 if half else code&0xFFFF).astype(jnp.float32)
                sc=s_sc[half,r:r+bc,c*LANES:(c+1)*LANES]+bias
                parts[half].append(jnp.where(valid[:,c*LANES:(c+1)*LANES],sc,masked_score))
        for half in range(2):
            ps=parts[half]
            m=ps[0]
            for x in ps[1:]: m=jnp.maximum(m,x)
            m=jnp.max(m,axis=1,keepdims=True)
            es=[jnp.exp((x-m)*(1.0/STEP)) for x in ps]
            tot=es[0]
            for x in es[1:]: tot=tot+x
            inv=1.0/jnp.sum(tot,axis=1,keepdims=True)
            pb=jnp.concatenate([x*inv for x in es],axis=1)
            if bc<rc:
                pb=jnp.concatenate([pb,jnp.zeros((rc-bc,span),jnp.float32)],axis=0)
            p_ref[half,r:r+rc,:]=pb.astype(jnp.bfloat16)
    acc=jnp.dot(p_ref[0],vz[0],preferred_element_type=jnp.float32)+jnp.dot(p_ref[1],vz[1],preferred_element_type=jnp.float32)
    mixed_ref[...]=acc[:length].astype(jnp.bfloat16)

def pack_tables(tables):
    fixed=jnp.round(jnp.transpose(tables,(2,0,1)).astype(jnp.float32)*STEP).astype(jnp.int32)
    return (fixed[1::2]<<16)+(fixed[0::2]+10240)

def attention_forward(q,k,v,buckets,mask_row,tables):
    length,width=q.shape
    heads=width//HEAD_DIM
    span=-(-length//LANES)*LANES
    tall=-(-length//16)*16
    packed=pack_tables(tables)
    col=lambda p:(0,p)
    return pl.pallas_call(partial(fwd_kernel,length),
        grid=(heads//2,),
        in_specs=[pl.BlockSpec((length,LANES),col),
            pl.BlockSpec((length,LANES),col),
            pl.BlockSpec((length,LANES),col),
            pl.BlockSpec((1,3,length,length),lambda p:(0,0,0,0)),
            pl.BlockSpec((1,span),lambda p:(0,0)),
            pl.BlockSpec((1,3,LANES),lambda p:(p,0,0))],
        out_specs=[pl.BlockSpec((length,LANES),col),pl.BlockSpec((2,tall,span),lambda p:(p,0,0))],
        out_shape=[jax.ShapeDtypeStruct((length,width),jnp.bfloat16),jax.ShapeDtypeStruct((heads,tall,span),jnp.bfloat16)],
        scratch_shapes=[pltpu.VMEM((2,span,LANES),jnp.bfloat16),pltpu.VMEM((2,span,LANES),jnp.bfloat16),pltpu.VMEM((tall,LANES),jnp.bfloat16),pltpu.VMEM((3,tall,LANES),jnp.int32),pltpu.VMEM((2,tall,span),jnp.float32)],
        compiler_params=pltpu.CompilerParams(vmem_limit_bytes=48*1024*1024),
        name="attn_fwd",
    )(q,k,v,buckets,mask_row,packed)


def bwd_kernel(length, q_ref, k_ref, v_ref, dm_ref, p_ref, dq_ref, dk_ref, dv_ref, ds_ref, kz, vz, qz, dz, dp_sc):
    pair=pl.program_id(0)
    span=kz.shape[1]
    tall=qz.shape[0]
    @pl.when(pair==0)
    def _():
        kz[...]=jnp.zeros_like(kz)
        vz[...]=jnp.zeros_like(vz)
        qz[...]=jnp.zeros_like(qz)
        dz[...]=jnp.zeros_like(dz)
    low=lax.broadcasted_iota(jnp.int32,(length,LANES),1)<HEAD_DIM
    kk=k_ref[...].astype(jnp.float32)*HEAD_DIM**-0.5
    vv=v_ref[...].astype(jnp.float32)
    kz[0,:length,:]=jnp.where(low,kk,0.0).astype(jnp.bfloat16)
    kz[1,:length,:]=jnp.where(low,0.0,kk).astype(jnp.bfloat16)
    vz[0,:length,:]=jnp.where(low,vv,0.0).astype(jnp.bfloat16)
    vz[1,:length,:]=jnp.where(low,0.0,vv).astype(jnp.bfloat16)
    qz[:length,:]=(q_ref[...].astype(jnp.float32)*HEAD_DIM**-0.5).astype(jnp.bfloat16)
    dz[:length,:]=dm_ref[...]
    for half in range(2):
        dp_sc[half]=lax.dot_general(dz[...],vz[half],(((1,),(1,)),((),())),preferred_element_type=jnp.float32)
    for half in range(2):
        for r in range(0,tall,RB):
            rc=min(RB,tall-r)
            p=p_ref[half,r:r+rc,:].astype(jnp.float32)
            dp=dp_sc[half,r:r+rc,:]
            delta=jnp.sum(p*dp,axis=1,keepdims=True)
            ds_ref[half,r:r+rc,:]=(p*(dp-delta)).astype(jnp.bfloat16)
    dq=jnp.dot(ds_ref[0],kz[0],preferred_element_type=jnp.float32)+jnp.dot(ds_ref[1],kz[1],preferred_element_type=jnp.float32)
    dq_ref[...]=dq[:length].astype(jnp.bfloat16)
    turned=(((0,),(0,)),((),()))
    grad=lambda left,right: lax.dot_general(left,right,turned,preferred_element_type=jnp.float32)[:length]
    dk_ref[...]=jnp.where(low,grad(ds_ref[0],qz[...]),grad(ds_ref[1],qz[...])).astype(jnp.bfloat16)
    dv_ref[...]=jnp.where(low,grad(p_ref[0],dz[...]),grad(p_ref[1],dz[...])).astype(jnp.bfloat16)

def attention_backward(q,k,v,dm,probs):
    length,width=q.shape
    heads,tall,span=probs.shape
    col=pl.BlockSpec((length,LANES),lambda p:(0,p))
    big=pl.BlockSpec((2,tall,span),lambda p:(p,0,0))
    flat=jax.ShapeDtypeStruct((length,width),jnp.bfloat16)
    return pl.pallas_call(partial(bwd_kernel,length),
        grid=(heads//2,),
        in_specs=[col,col,col,col,big],
        out_specs=[col,col,col,big],
        out_shape=[flat,flat,flat,jax.ShapeDtypeStruct(probs.shape,jnp.bfloat16)],
        scratch_shapes=[pltpu.VMEM((2,span,LANES),jnp.bfloat16),pltpu.VMEM((2,span,LANES),jnp.bfloat16),pltpu.VMEM((tall,LANES),jnp.bfloat16),pltpu.VMEM((tall,LANES),jnp.bfloat16),pltpu.VMEM((2,tall,span),jnp.float32)],
        compiler_params=pltpu.CompilerParams(vmem_limit_bytes=48*1024*1024),
        name="attn_bwd",
    )(q,k,v,dm,probs)

TQ=32
GROUP=2
HIGH=4
def table_kernel(length, heads, ds_ref, b_ref, o_ref, dt, tail, acc):
    step=pl.program_id(0)
    span=ds_ref.shape[2]
    full=length//LANES
    rest=length-full*LANES
    low_count=LANES//HIGH
    @pl.when(step==0)
    def _():
        acc[...]=jnp.zeros_like(acc)
        tail[...]=jnp.zeros_like(tail)
        if heads<8:
            dt[...]=jnp.zeros_like(dt)
    for t in range(3):
        tail[t,:,:rest]=b_ref[0,t,:,full*LANES:]
    for h in range(heads):
        for c in range(span//LANES):
            dt[c,pl.ds(h,TQ,8),:]=ds_ref[h,:,c*LANES:(c+1)*LANES].astype(jnp.float32)
    ladder=lax.broadcasted_iota(jnp.int32,(8,LANES),0)
    for i0 in range(0,TQ,GROUP):
        lefts=[[] for _ in range(3*HIGH)]
        rights=[[] for _ in range(3*low_count//8)]
        for i in range(i0,i0+GROUP):
            for c in range(span//LANES):
                d8=dt[c,i*8:(i+1)*8,:]
                for t in range(3):
                    row=b_ref[0,t,i:i+1,c*LANES:(c+1)*LANES] if c<full else tail[t,i:i+1,:]
                    row=jnp.broadcast_to(row,(8,LANES))
                    high=lax.shift_right_logical(row,low_count.bit_length()-1)
                    low=(row&(low_count-1))-ladder
                    for m in range(HIGH):
                        lefts[t*HIGH+m].append(jnp.where(high==m,d8,0.0))
                    for m in range(low_count//8):
                        rights[t*(low_count//8)+m].append(jnp.where(low==8*m,1.0,0.0))
        left=jnp.concatenate([jnp.concatenate(x,axis=1) for x in lefts],axis=0).astype(jnp.bfloat16)
        right=jnp.concatenate([jnp.concatenate(x,axis=1) for x in rights],axis=0).astype(jnp.bfloat16)
        acc[...]+=lax.dot_general(left,right,(((1,),(1,)),((),())),preferred_element_type=jnp.float32)
    o_ref[...]=acc[...]

def table_grads(ds,buckets):
    heads,tall,span=ds.shape
    length=buckets.shape[2]
    low_count=LANES//HIGH
    out=pl.pallas_call(partial(table_kernel,length,heads),
        grid=(-(-tall//TQ),),
        in_specs=[pl.BlockSpec((heads,TQ,span),lambda i:(0,i,0)),pl.BlockSpec((1,3,TQ,length),lambda i:(0,0,i,0))],
        out_specs=pl.BlockSpec((24*HIGH,3*low_count),lambda i:(0,0)),
        out_shape=jax.ShapeDtypeStruct((24*HIGH,3*low_count),jnp.float32),
        scratch_shapes=[pltpu.VMEM((span//LANES,TQ*8,LANES),jnp.float32),pltpu.VMEM((3,TQ,LANES),jnp.int32),pltpu.VMEM((24*HIGH,3*low_count),jnp.float32)],
        compiler_params=pltpu.CompilerParams(vmem_limit_bytes=48*1024*1024),
        name="table_grads",
    )(ds,buckets)
    own=jnp.stack([out[t*8*HIGH:(t+1)*8*HIGH,t*low_count:(t+1)*low_count] for t in range(3)])
    own=own.reshape(3,HIGH,8,low_count)[:,:,:heads]
    return jnp.transpose(own,(0,1,3,2)).reshape(3,LANES,heads)


def norm_forward(values, gain, shift, row_total, width):
    pair_sums = row_total((jnp.sum(values, axis=-1), jnp.sum(values * values, axis=-1)))
    center = pair_sums[0] / width
    spread = pair_sums[1] / width - center * center
    scaling = lax.rsqrt(spread + norm_epsilon)
    normal = (values - center[:, None]) * scaling[:, None]
    return (normal * gain + shift, normal, scaling)


def norm_backward(grad_out, normal, scaling, gain, row_total, width):
    scaled = grad_out * gain
    pair_sums = row_total((jnp.sum(scaled, axis=-1), jnp.sum(scaled * normal, axis=-1)))
    return scaling[:, None] * (
        scaled - pair_sums[0][:, None] / width - normal * (pair_sums[1][:, None] / width)
    )


def body(
    tokens,
    qkv_weight,
    qv_bias,
    out_weight,
    out_bias,
    up_weight,
    up_bias,
    down_weight,
    down_bias,
    norm_gain,
    norm_shift,
    rel_tables,
    buckets,
    key_mask,
    cotangent,
):
    width = tokens.shape[1]
    row_count = tokens.shape[0]
    share = width // lax.axis_size("tensor")
    offset = lax.axis_index("tensor") * share
    pages = buckets.shape[0]
    length = buckets.shape[2]
    local_width = qkv_weight.shape[2]

    def own_columns(matrix):
        return lax.dynamic_slice_in_dim(matrix, offset, share, matrix.ndim - 1)

    def branch_total(summand):
        return lax.psum_scatter(
            summand.astype(jnp.bfloat16), "tensor", scatter_dimension=1, tiled=True
        ).astype(jnp.float32)

    def row_total(row_pair):
        return lax.psum(row_pair, "tensor")

    def full_width(narrow_rows):
        return lax.all_gather(narrow_rows, "tensor", axis=1, tiled=True)

    def local_cols(matrix):
        return own_columns(matrix)

    grad_rows = cotangent.astype(jnp.float32)
    projected = jnp.einsum("td,dce->tce", tokens, qkv_weight, preferred_element_type=jnp.float32)
    queries = (projected[:, 0] + qv_bias[0].astype(jnp.float32)).astype(jnp.bfloat16)
    keys_all = projected[:, 1].astype(jnp.bfloat16)
    values_all = (projected[:, 2] + qv_bias[1].astype(jnp.float32)).astype(jnp.bfloat16)
    span = -(-length // LANES) * LANES
    mask_rows = jnp.pad(key_mask, ((0, 0), (0, span - length)))

    def page_of(matrix, page):
        return matrix[page * length : (page + 1) * length]

    forward = [
        attention_forward(
            page_of(queries, page),
            page_of(keys_all, page),
            page_of(values_all, page),
            buckets[page : page + 1],
            mask_rows[page : page + 1],
            rel_tables,
        )
        for page in range(pages)
    ]
    mixed = jnp.concatenate([mixed_page for mixed_page, _ in forward])
    attn_term = jnp.dot(mixed, out_weight, preferred_element_type=jnp.float32)
    gains = norm_gain.astype(jnp.float32)
    shifts = norm_shift.astype(jnp.float32)
    first = local_cols(tokens).astype(jnp.float32) + (
        branch_total(attn_term) + local_cols(out_bias).astype(jnp.float32)
    )
    normed, normal_one, scaling_one = norm_forward(
        first, local_cols(gains[0]), local_cols(shifts[0]), row_total, width
    )
    normed_low = full_width(normed.astype(jnp.bfloat16))
    pre_act = jnp.dot(normed_low, up_weight, preferred_element_type=jnp.float32) + up_bias.astype(
        jnp.float32
    )
    hidden, gelu_pull = jax.vjp(exact_gelu, pre_act)
    hidden_low = hidden.astype(jnp.bfloat16)
    ffn_term = jnp.dot(hidden_low, down_weight, preferred_element_type=jnp.float32)
    second = normed + (branch_total(ffn_term) + local_cols(down_bias).astype(jnp.float32))
    result, normal_two, scaling_two = norm_forward(
        second, local_cols(gains[1]), local_cols(shifts[1]), row_total, width
    )
    layer_out = result.astype(jnp.bfloat16)
    grad_gain_two = jnp.sum(grad_rows * normal_two, axis=0)
    grad_shift_two = jnp.sum(grad_rows, axis=0)
    grad_second = norm_backward(
        grad_rows, normal_two, scaling_two, local_cols(gains[1]), row_total, width
    )
    grad_ffn = grad_second.astype(jnp.bfloat16)
    grad_down_bias = jnp.sum(grad_ffn.astype(jnp.float32), axis=0)
    grad_ffn_full = full_width(grad_ffn)
    grad_down_weight = jnp.einsum(
        "tf,td->fd", hidden_low, grad_ffn_full, preferred_element_type=jnp.float32
    )
    grad_hidden = jnp.einsum(
        "td,fd->tf", grad_ffn_full, down_weight, preferred_element_type=jnp.float32
    )
    grad_pre = gelu_pull(grad_hidden)[0].astype(jnp.bfloat16)
    grad_up_bias = jnp.sum(grad_pre.astype(jnp.float32), axis=0)
    grad_up_weight = jnp.einsum(
        "td,tf->df", normed_low, grad_pre, preferred_element_type=jnp.float32
    )
    grad_normed = grad_second + branch_total(
        jnp.einsum("tf,df->td", grad_pre, up_weight, preferred_element_type=jnp.float32)
    )
    grad_gain_one = jnp.sum(grad_normed * normal_one, axis=0)
    grad_shift_one = jnp.sum(grad_normed, axis=0)
    grad_first = norm_backward(
        grad_normed, normal_one, scaling_one, local_cols(gains[0]), row_total, width
    )
    grad_attended = grad_first.astype(jnp.bfloat16)
    grad_out_bias = jnp.sum(grad_attended.astype(jnp.float32), axis=0)
    grad_attended_full = full_width(grad_attended)
    grad_out_weight = jnp.einsum(
        "te,td->ed", mixed, grad_attended_full, preferred_element_type=jnp.float32
    )
    grad_mixed = jnp.einsum(
        "td,ed->te", grad_attended_full, out_weight, preferred_element_type=jnp.float32
    ).astype(jnp.bfloat16)
    backward = [
        attention_backward(
            page_of(queries, page),
            page_of(keys_all, page),
            page_of(values_all, page),
            page_of(grad_mixed, page),
            forward[page][1],
        )
        for page in range(pages)
    ]
    grad_queries, grad_keys, grad_values = (
        jnp.concatenate([parts[which] for parts in backward]) for which in range(3)
    )
    grad_rel_tables = sum(
        table_grads(backward[page][3], buckets[page : page + 1]) for page in range(pages)
    )
    grad_stack = jnp.stack([grad_queries, grad_keys, grad_values], axis=1)
    grad_qkv_weight = jnp.einsum(
        "td,tce->dce", tokens, grad_stack, preferred_element_type=jnp.float32
    )
    grad_qv_bias = jnp.stack(
        [
            jnp.sum(grad_queries.astype(jnp.float32), axis=0),
            jnp.sum(grad_values.astype(jnp.float32), axis=0),
        ]
    )
    input_term = jnp.einsum(
        "tce,dce->td", grad_stack, qkv_weight, preferred_element_type=jnp.float32
    )
    grad_tokens = (
        lax.psum_scatter(
            input_term.astype(jnp.bfloat16), "tensor", scatter_dimension=1, tiled=True
        ).astype(jnp.float32)
        + grad_first
    ).astype(jnp.bfloat16)
    (
        grad_qkv_weight,
        grad_qv_bias,
        grad_out_weight,
        grad_out_bias,
        grad_rel_tables,
        grad_gain_one,
        grad_shift_one,
        grad_up_weight,
        grad_up_bias,
        grad_down_weight,
        grad_down_bias,
        grad_gain_two,
        grad_shift_two,
    ) = (
        lax.psum(grad_qkv_weight.astype(jnp.bfloat16), "dp").astype(jnp.float32),
        lax.psum(grad_qv_bias.astype(jnp.bfloat16), "dp").astype(jnp.float32),
        lax.psum(grad_out_weight.astype(jnp.bfloat16), "dp").astype(jnp.float32),
        lax.psum(grad_out_bias.astype(jnp.bfloat16), "dp").astype(jnp.float32),
        lax.psum(grad_rel_tables.astype(jnp.bfloat16), "dp").astype(jnp.float32),
        lax.psum(grad_gain_one.astype(jnp.bfloat16), "dp").astype(jnp.float32),
        lax.psum(grad_shift_one.astype(jnp.bfloat16), "dp").astype(jnp.float32),
        lax.psum(grad_up_weight.astype(jnp.bfloat16), "dp").astype(jnp.float32),
        lax.psum(grad_up_bias.astype(jnp.bfloat16), "dp").astype(jnp.float32),
        lax.psum(grad_down_weight.astype(jnp.bfloat16), "dp").astype(jnp.float32),
        lax.psum(grad_down_bias.astype(jnp.bfloat16), "dp").astype(jnp.float32),
        lax.psum(grad_gain_two.astype(jnp.bfloat16), "dp").astype(jnp.float32),
        lax.psum(grad_shift_two.astype(jnp.bfloat16), "dp").astype(jnp.float32),
    )
    grad_norm_gain = jnp.stack([grad_gain_one, grad_gain_two])
    grad_norm_shift = jnp.stack([grad_shift_one, grad_shift_two])
    return (
        layer_out,
        grad_tokens,
        grad_qkv_weight,
        grad_qv_bias,
        grad_out_weight,
        grad_out_bias,
        grad_up_weight,
        grad_up_bias,
        grad_down_weight,
        grad_down_bias,
        grad_norm_gain,
        grad_norm_shift,
        grad_rel_tables,
    )


def solution(mesh):
    in_specs = (
        P("dp", None),
        P(None, None, "tensor"),
        P(None, "tensor"),
        P("tensor", None),
        P(),
        P(None, "tensor"),
        P("tensor"),
        P("tensor", None),
        P(),
        P(),
        P(),
        P(None, None, "tensor"),
        P("dp", None, None, None),
        P("dp", None),
        P("dp", "tensor"),
    )
    out_specs = (
        P("dp", "tensor"),
        P("dp", "tensor"),
        P(None, None, "tensor"),
        P(None, "tensor"),
        P("tensor", None),
        P("tensor"),
        P(None, "tensor"),
        P("tensor"),
        P("tensor", None),
        P("tensor"),
        P(None, "tensor"),
        P(None, "tensor"),
        P(None, None, "tensor"),
    )
    return jax.shard_map(body, mesh=mesh, in_specs=in_specs, out_specs=out_specs, check_vma=False)
```

```python
from functools import partial

import jax
import jax.numpy as jnp
from jax import lax
from jax.experimental import pallas as pl
from jax.experimental.pallas import tpu as pltpu
from jax.sharding import PartitionSpec as P

HEAD_DIM = 64


norm_epsilon = 1e-05
masked_score = -1e30


def exact_gelu(values):
    return jax.nn.gelu(values, approximate=False)


LANES = 128
STEP = 2048.0
RC = 576
RB = 96


def fwd_kernel(length, q_ref, k_ref, v_ref, b_ref, m_ref, t_ref, mixed_ref, p_ref, kz, vz, qz, tail, s_sc):
    pair=pl.program_id(0)
    span=kz.shape[1]
    tall=qz.shape[0]
    full=length//LANES
    rest=length-full*LANES
    @pl.when(pair==0)
    def _():
        kz[...]=jnp.zeros_like(kz)
        vz[...]=jnp.zeros_like(vz)
        qz[...]=jnp.zeros_like(qz)
        tail[...]=jnp.zeros_like(tail)
        for t in range(3):
            tail[t,:length,:rest]=b_ref[0,t,:,full*LANES:]
    low=lax.broadcasted_iota(jnp.int32,(length,LANES),1)<HEAD_DIM
    kk=k_ref[...].astype(jnp.float32)*(HEAD_DIM**-0.5*STEP)
    vv=v_ref[...].astype(jnp.float32)
    kz[0,:length,:]=jnp.where(low,kk,0.0).astype(jnp.bfloat16)
    kz[1,:length,:]=jnp.where(low,0.0,kk).astype(jnp.bfloat16)
    vz[0,:length,:]=jnp.where(low,vv,0.0).astype(jnp.bfloat16)
    vz[1,:length,:]=jnp.where(low,0.0,vv).astype(jnp.bfloat16)
    qz[:length,:]=q_ref[...]
    valid=m_ref[...]>0
    for half in range(2):
        s_sc[half]=lax.dot_general(qz[...],kz[half],(((1,),(1,)),((),())),preferred_element_type=jnp.float32)
    for r in range(0,tall,RC):
        rc=min(RC,tall-r)
        bc=min(rc,length-r)
        tabs=[jnp.broadcast_to(t_ref[0,t:t+1,:],(bc,LANES)) for t in range(3)]
        parts=[[],[]]
        for c in range(span//LANES):
            code=None
            for t in range(3):
                idx=(b_ref[0,t,r:r+bc,c*LANES:(c+1)*LANES] if c<full else tail[t,r:r+bc,:])
                g=jnp.take_along_axis(tabs[t],idx,axis=1,mode="promise_in_bounds")
                code=g if code is None else code+g
            for half in range(2):
                bias=(code>>16 if half else code&0xFFFF).astype(jnp.float32)
                sc=s_sc[half,r:r+bc,c*LANES:(c+1)*LANES]+bias
                parts[half].append(jnp.where(valid[:,c*LANES:(c+1)*LANES],sc,masked_score))
        for half in range(2):
            ps=parts[half]
            m=ps[0]
            for x in ps[1:]: m=jnp.maximum(m,x)
            m=jnp.max(m,axis=1,keepdims=True)
            es=[jnp.exp((x-m)*(1.0/STEP)) for x in ps]
            tot=es[0]
            for x in es[1:]: tot=tot+x
            inv=1.0/jnp.sum(tot,axis=1,keepdims=True)
            pb=jnp.concatenate([x*inv for x in es],axis=1)
            if bc<rc:
                pb=jnp.concatenate([pb,jnp.zeros((rc-bc,span),jnp.float32)],axis=0)
            p_ref[half,r:r+rc,:]=pb.astype(jnp.bfloat16)
    acc=jnp.dot(p_ref[0],vz[0],preferred_element_type=jnp.float32)+jnp.dot(p_ref[1],vz[1],preferred_element_type=jnp.float32)
    mixed_ref[...]=acc[:length].astype(jnp.bfloat16)

def pack_tables(tables):
    fixed=jnp.round(jnp.transpose(tables,(2,0,1)).astype(jnp.float32)*STEP).astype(jnp.int32)
    return (fixed[1::2]<<16)+(fixed[0::2]+10240)

def attention_forward(q,k,v,buckets,mask_row,tables,at,heads):
    length=q.shape[0]
    width=heads*HEAD_DIM
    packed=pack_tables(tables)
    own=pl.BlockSpec((length,LANES),lambda p:(0,p+at))
    span=-(-length//LANES)*LANES
    tall=-(-length//16)*16
    col=lambda p:(0,p)
    return pl.pallas_call(partial(fwd_kernel,length),
        grid=(heads//2,),
        in_specs=[own,
            own,
            own,
            pl.BlockSpec((1,3,length,length),lambda p:(0,0,0,0)),
            pl.BlockSpec((1,span),lambda p:(0,0)),
            pl.BlockSpec((1,3,LANES),lambda p:(p+at,0,0))],
        out_specs=[pl.BlockSpec((length,LANES),col),pl.BlockSpec((2,tall,span),lambda p:(p,0,0))],
        out_shape=[jax.ShapeDtypeStruct((length,width),jnp.bfloat16),jax.ShapeDtypeStruct((heads,tall,span),jnp.bfloat16)],
        scratch_shapes=[pltpu.VMEM((2,span,LANES),jnp.bfloat16),pltpu.VMEM((2,span,LANES),jnp.bfloat16),pltpu.VMEM((tall,LANES),jnp.bfloat16),pltpu.VMEM((3,tall,LANES),jnp.int32),pltpu.VMEM((2,tall,span),jnp.float32)],
        compiler_params=pltpu.CompilerParams(vmem_limit_bytes=48*1024*1024),
        name="attn_fwd",
    )(q,k,v,buckets,mask_row,packed)


def bwd_kernel(length, q_ref, k_ref, v_ref, dm_ref, p_ref, dq_ref, dk_ref, dv_ref, ds_ref, kz, vz, qz, dz, dp_sc):
    pair=pl.program_id(0)
    span=kz.shape[1]
    tall=qz.shape[0]
    @pl.when(pair==0)
    def _():
        kz[...]=jnp.zeros_like(kz)
        vz[...]=jnp.zeros_like(vz)
        qz[...]=jnp.zeros_like(qz)
        dz[...]=jnp.zeros_like(dz)
    low=lax.broadcasted_iota(jnp.int32,(length,LANES),1)<HEAD_DIM
    kk=k_ref[...].astype(jnp.float32)*HEAD_DIM**-0.5
    vv=v_ref[...].astype(jnp.float32)
    kz[0,:length,:]=jnp.where(low,kk,0.0).astype(jnp.bfloat16)
    kz[1,:length,:]=jnp.where(low,0.0,kk).astype(jnp.bfloat16)
    vz[0,:length,:]=jnp.where(low,vv,0.0).astype(jnp.bfloat16)
    vz[1,:length,:]=jnp.where(low,0.0,vv).astype(jnp.bfloat16)
    qz[:length,:]=(q_ref[...].astype(jnp.float32)*HEAD_DIM**-0.5).astype(jnp.bfloat16)
    dz[:length,:]=dm_ref[...]
    for half in range(2):
        dp_sc[half]=lax.dot_general(dz[...],vz[half],(((1,),(1,)),((),())),preferred_element_type=jnp.float32)
    for half in range(2):
        for r in range(0,tall,RB):
            rc=min(RB,tall-r)
            p=p_ref[half,r:r+rc,:].astype(jnp.float32)
            dp=dp_sc[half,r:r+rc,:]
            delta=jnp.sum(p*dp,axis=1,keepdims=True)
            ds_ref[half,r:r+rc,:]=(p*(dp-delta)).astype(jnp.bfloat16)
    dq=jnp.dot(ds_ref[0],kz[0],preferred_element_type=jnp.float32)+jnp.dot(ds_ref[1],kz[1],preferred_element_type=jnp.float32)
    dq_ref[...]=dq[:length].astype(jnp.bfloat16)
    turned=(((0,),(0,)),((),()))
    grad=lambda left,right: lax.dot_general(left,right,turned,preferred_element_type=jnp.float32)[:length]
    dk_ref[...]=jnp.where(low,grad(ds_ref[0],qz[...]),grad(ds_ref[1],qz[...])).astype(jnp.bfloat16)
    dv_ref[...]=jnp.where(low,grad(p_ref[0],dz[...]),grad(p_ref[1],dz[...])).astype(jnp.bfloat16)

def attention_backward(q,k,v,dm,probs,at):
    length=q.shape[0]
    heads,tall,span=probs.shape
    width=heads*HEAD_DIM
    col=pl.BlockSpec((length,LANES),lambda p:(0,p))
    own=pl.BlockSpec((length,LANES),lambda p:(0,p+at))
    big=pl.BlockSpec((2,tall,span),lambda p:(p,0,0))
    flat=jax.ShapeDtypeStruct((length,width),jnp.bfloat16)
    return pl.pallas_call(partial(bwd_kernel,length),
        grid=(heads//2,),
        in_specs=[own,own,own,own,big],
        out_specs=[col,col,col,big],
        out_shape=[flat,flat,flat,jax.ShapeDtypeStruct(probs.shape,jnp.bfloat16)],
        scratch_shapes=[pltpu.VMEM((2,span,LANES),jnp.bfloat16),pltpu.VMEM((2,span,LANES),jnp.bfloat16),pltpu.VMEM((tall,LANES),jnp.bfloat16),pltpu.VMEM((tall,LANES),jnp.bfloat16),pltpu.VMEM((2,tall,span),jnp.float32)],
        compiler_params=pltpu.CompilerParams(vmem_limit_bytes=48*1024*1024),
        name="attn_bwd",
    )(q,k,v,dm,probs)

TQ=32
GROUP=2
HIGH=4
def table_kernel(length, count, *refs):
    ds_refs,(b_ref,o_ref,dt,tail,acc)=refs[:count],refs[count:]
    step=pl.program_id(0)
    span=ds_refs[0].shape[2]
    heads=sum(ref.shape[0] for ref in ds_refs)
    full=length//LANES
    rest=length-full*LANES
    low_count=LANES//HIGH
    @pl.when(step==0)
    def _():
        acc[...]=jnp.zeros_like(acc)
        tail[...]=jnp.zeros_like(tail)
        if heads<8:
            dt[...]=jnp.zeros_like(dt)
    for t in range(3):
        tail[t,:,:rest]=b_ref[0,t,:,full*LANES:]
    h=0
    for ref in ds_refs:
        for inner in range(ref.shape[0]):
            for c in range(span//LANES):
                dt[c,pl.ds(h,TQ,8),:]=ref[inner,:,c*LANES:(c+1)*LANES].astype(jnp.float32)
            h+=1
    ladder=lax.broadcasted_iota(jnp.int32,(8,LANES),0)
    for i0 in range(0,TQ,GROUP):
        lefts=[[] for _ in range(3*HIGH)]
        rights=[[] for _ in range(3*low_count//8)]
        for i in range(i0,i0+GROUP):
            for c in range(span//LANES):
                d8=dt[c,i*8:(i+1)*8,:]
                for t in range(3):
                    row=b_ref[0,t,i:i+1,c*LANES:(c+1)*LANES] if c<full else tail[t,i:i+1,:]
                    row=jnp.broadcast_to(row,(8,LANES))
                    high=lax.shift_right_logical(row,low_count.bit_length()-1)
                    low=(row&(low_count-1))-ladder
                    for m in range(HIGH):
                        lefts[t*HIGH+m].append(jnp.where(high==m,d8,0.0))
                    for m in range(low_count//8):
                        rights[t*(low_count//8)+m].append(jnp.where(low==8*m,1.0,0.0))
        left=jnp.concatenate([jnp.concatenate(x,axis=1) for x in lefts],axis=0).astype(jnp.bfloat16)
        right=jnp.concatenate([jnp.concatenate(x,axis=1) for x in rights],axis=0).astype(jnp.bfloat16)
        acc[...]+=lax.dot_general(left,right,(((1,),(1,)),((),())),preferred_element_type=jnp.float32)
    o_ref[...]=acc[...]

def table_grads(ds,buckets):
    heads=sum(each.shape[0] for each in ds)
    _,tall,span=ds[0].shape
    length=buckets.shape[2]
    low_count=LANES//HIGH
    out=pl.pallas_call(partial(table_kernel,length,len(ds)),
        grid=(-(-tall//TQ),),
        in_specs=[pl.BlockSpec((each.shape[0],TQ,span),lambda i:(0,i,0)) for each in ds]+[pl.BlockSpec((1,3,TQ,length),lambda i:(0,0,i,0))],
        out_specs=pl.BlockSpec((24*HIGH,3*low_count),lambda i:(0,0)),
        out_shape=jax.ShapeDtypeStruct((24*HIGH,3*low_count),jnp.float32),
        scratch_shapes=[pltpu.VMEM((span//LANES,TQ*8,LANES),jnp.float32),pltpu.VMEM((3,TQ,LANES),jnp.int32),pltpu.VMEM((24*HIGH,3*low_count),jnp.float32)],
        compiler_params=pltpu.CompilerParams(vmem_limit_bytes=48*1024*1024),
        name="table_grads",
    )(*ds,buckets)
    own=jnp.stack([out[t*8*HIGH:(t+1)*8*HIGH,t*low_count:(t+1)*low_count] for t in range(3)])
    own=own.reshape(3,HIGH,8,low_count)[:,:,:heads]
    return jnp.transpose(own,(0,1,3,2)).reshape(3,LANES,heads)


def rows_cut(length):
    first = -(-length // 32) * 16
    return ((0, first), (first, length)) if first < length else ((0, length),)


def norm_forward(values, gain, shift):
    width = values.shape[1]
    center = jnp.sum(values, axis=-1, keepdims=True) / width
    deviation = values - center
    spread = jnp.sum(deviation * deviation, axis=-1, keepdims=True) / width
    scaling = lax.rsqrt(spread + norm_epsilon)
    normal = deviation * scaling
    return normal * gain + shift, normal, scaling


def norm_backward(grad_out, normal, scaling, gain):
    width = grad_out.shape[1]
    scaled = grad_out * gain
    first = jnp.sum(scaled, axis=-1, keepdims=True) / width
    second = jnp.sum(scaled * normal, axis=-1, keepdims=True) / width
    return scaling * (scaled - first - normal * second)


def dot_to(left, right, dims=((1,), (0,))):
    return lax.dot_general(left, right, (dims, ((), ())), preferred_element_type=jnp.float32)


def page_place(which):
    return lax.axis_index("dp") // {"core": 1, "y": 2, "z": 4}[which] % (4 if which == "z" else 2)


def move(matrix, partner, senders=range(4)):
    return lax.ppermute(
        matrix, "dp", [(i, partner(i)) for i in range(16) if i // 4 in senders]
    )


def over_core(i):
    return i ^ 1


def over_y(i):
    return i ^ 2


def over_z(i):
    return i ^ 4


def across_z(i):
    return 12 - i // 4 * 4 + i % 4


def added(left, right):
    return (left.astype(jnp.float32) + right.astype(jnp.float32)).astype(jnp.bfloat16)


def half_of(matrix, which):
    count = matrix.shape[0] // 2
    return lax.dynamic_slice_in_dim(matrix, which * count, count, 0)


def half_total(matrix, partner, which):
    return added(half_of(matrix, which), move(half_of(matrix, 1 - which), partner))


def both_halves(matrix, partner, which):
    other = move(matrix, partner)
    return jnp.concatenate(
        [jnp.where(which == 0, matrix, other), jnp.where(which == 0, other, matrix)]
    )


def along_z(matrix):
    z = page_place("z")
    matrix = added(matrix, move(matrix, over_z, (0, 3)))
    matrix = added(matrix, move(matrix, across_z, (1, 2)))
    other = move(matrix, over_z, (1, 2))
    return jnp.where((z == 0) | (z == 3), other, matrix)


def page_totals(matrices):
    if lax.axis_size("dp") != 16:
        return lax.psum(tuple(matrices), "dp")
    core, y = page_place("core"), page_place("y")
    totals = []
    for matrix in matrices:
        mine = half_total(matrix, over_core, core)
        parts = 2 if mine.shape[1] > 1024 else 1
        columns = mine.shape[1] // parts
        done = [
            both_halves(
                along_z(half_total(mine[:, at * columns : (at + 1) * columns], over_y, y)),
                over_y,
                y,
            )
            for at in range(parts)
        ]
        totals.append(both_halves(jnp.concatenate(done, axis=1), over_core, core))
    return totals


def small_total(packed):
    if lax.axis_size("dp") != 16:
        return lax.psum(packed, "dp")
    for partner in (lambda i: i ^ 1, lambda i: i ^ 2, lambda i: i ^ 4, lambda i: 12 - (i & 12) | (i & 3)):
        packed = packed + lax.ppermute(packed, "dp", [(i, partner(i)) for i in range(16)])
    return packed


def body(
    tokens,
    qkv_weight,
    qv_bias,
    out_weight,
    out_bias,
    up_weight,
    up_bias,
    down_weight,
    down_bias,
    norm_gain,
    norm_shift,
    rel_tables,
    buckets,
    key_mask,
    cotangent,
):
    single = jnp.float32
    low = jnp.bfloat16
    shares = lax.axis_size("tensor")
    place = lax.axis_index("tensor")
    width = tokens.shape[1]
    share = width // shares
    pages, _, length, _ = buckets.shape
    local_width = qkv_weight.shape[2]

    def own_columns(matrix):
        return lax.dynamic_slice_in_dim(matrix, place * share, share, matrix.ndim - 1)

    def swap(matrix):
        return lax.ppermute(matrix, "tensor", [(0, 1), (1, 0)])

    def branch_total(summand):
        mine = summand.astype(low)
        if shares == 2:
            return mine.astype(single) + swap(mine).astype(single)
        return lax.psum(mine, "tensor").astype(single)

    if shares == 2:
        other = swap(cotangent)
        grad_rows = jnp.where(
            place == 0,
            jnp.concatenate([cotangent, other], axis=1),
            jnp.concatenate([other, cotangent], axis=1),
        )
        out_all = jnp.concatenate([out_weight, swap(out_weight)], axis=0)
    else:
        grad_rows = lax.all_gather(cotangent, "tensor", axis=1, tiled=True)

    projected = jnp.einsum("td,dce->tce", tokens, qkv_weight, preferred_element_type=single)
    queries = (projected[:, 0] + qv_bias[0].astype(single)).astype(low)
    keys_all = projected[:, 1].astype(low)
    values_all = (projected[:, 2] + qv_bias[1].astype(single)).astype(low)

    span = -(-length // LANES) * LANES
    mask_rows = jnp.pad(key_mask, ((0, 0), (0, span - length)))
    pairs = local_width // LANES
    groups = 2 if pairs % 2 == 0 else 1
    group_width = local_width // groups
    mixed_groups = []
    probs = []
    for group in range(groups):
        done = [
            attention_forward(
                queries[page * length : (page + 1) * length],
                keys_all[page * length : (page + 1) * length],
                values_all[page * length : (page + 1) * length],
                buckets[page : page + 1],
                mask_rows[page : page + 1],
                rel_tables,
                group * group_width // LANES,
                group_width // HEAD_DIM,
            )
            for page in range(pages)
        ]
        mixed_groups.append(jnp.concatenate([each[0] for each in done]))
        probs.append([each[1] for each in done])
    mixed = jnp.concatenate(mixed_groups, axis=1)
    if shares == 2:
        mixed_all = jnp.concatenate(mixed_groups + [swap(each) for each in mixed_groups], axis=1)
        attended = dot_to(mixed_all, out_all)
    else:
        attended = branch_total(dot_to(mixed, out_weight))

    gains = norm_gain.astype(single)
    shifts = norm_shift.astype(single)
    first = tokens.astype(single) + (attended + out_bias.astype(single))
    normed, normal_one, scaling_one = norm_forward(first, gains[0], shifts[0])
    normed_low = normed.astype(low)

    cuts = rows_cut(tokens.shape[0])
    slopes = []
    hidden_parts = []
    totals = []
    for start, stop in cuts:
        pre_act = dot_to(normed_low[start:stop], up_weight) + up_bias.astype(single)
        hidden, gelu_pull = jax.vjp(exact_gelu, pre_act)
        hidden_parts.append(hidden.astype(low))
        slopes.append(gelu_pull)
        totals.append(branch_total(dot_to(hidden_parts[-1], down_weight)))
    outs = []
    grad_ffn_parts = []
    grad_pre_parts = []
    grad_second_parts = []
    normal_two_parts = []
    branch = []
    for at, (start, stop) in enumerate(cuts):
        second = normed[start:stop] + (totals[at] + down_bias.astype(single))
        result, normal_two, scaling_two = norm_forward(second, gains[1], shifts[1])
        outs.append(own_columns(result.astype(low)))
        normal_two_parts.append(normal_two)
        grad_second = norm_backward(
            grad_rows[start:stop].astype(single), normal_two, scaling_two, gains[1]
        )
        grad_second_parts.append(grad_second)
        grad_ffn = grad_second.astype(low)
        grad_ffn_parts.append(grad_ffn)
        grad_hidden = dot_to(grad_ffn, down_weight, ((1,), (1,)))
        grad_pre = slopes[at](grad_hidden)[0].astype(low)
        grad_pre_parts.append(grad_pre)
        branch.append(branch_total(dot_to(grad_pre, up_weight, ((1,), (1,)))))
    layer_out = jnp.concatenate(outs)
    grad_ffn = jnp.concatenate(grad_ffn_parts)
    grad_pre = jnp.concatenate(grad_pre_parts)
    hidden_low = jnp.concatenate(hidden_parts)
    over_rows = ((0,), (0,))
    grad_down_weight = dot_to(hidden_low, grad_ffn, over_rows).astype(low)
    grad_up_weight = dot_to(normed_low, grad_pre, over_rows).astype(low)
    first_totals = lax.psum((grad_down_weight, grad_up_weight), "dp")

    grad_normed = jnp.concatenate(
        [part + more for part, more in zip(grad_second_parts, branch)]
    )
    grad_first = norm_backward(grad_normed, normal_one, scaling_one, gains[0])
    grad_attended = grad_first.astype(low)
    grad_mixed = dot_to(grad_attended, out_weight, ((1,), (1,))).astype(low)

    grad_query_parts = []
    grad_key_parts = []
    grad_value_parts = []
    table_parts = []
    score_grads = []
    for group in range(groups):
        done = [
            attention_backward(
                queries[page * length : (page + 1) * length],
                keys_all[page * length : (page + 1) * length],
                values_all[page * length : (page + 1) * length],
                grad_mixed[page * length : (page + 1) * length],
                probs[group][page],
                group * group_width // LANES,
            )
            for page in range(pages)
        ]
        grad_query_parts.append(jnp.concatenate([each[0] for each in done]))
        grad_key_parts.append(jnp.concatenate([each[1] for each in done]))
        grad_value_parts.append(jnp.concatenate([each[2] for each in done]))
        score_grads.append([each[3] for each in done])
    grad_queries = jnp.concatenate(grad_query_parts, axis=1)
    grad_keys = jnp.concatenate(grad_key_parts, axis=1)
    grad_values = jnp.concatenate(grad_value_parts, axis=1)
    grad_stack = jnp.concatenate([grad_queries, grad_keys, grad_values], axis=1)
    qkv_flat = qkv_weight.reshape(width, 3 * local_width)
    grad_out_weight = dot_to(mixed, grad_attended, over_rows).astype(low)
    grad_qkv_weight = dot_to(tokens, grad_stack, over_rows).astype(low)
    last_totals = page_totals([grad_qkv_weight, grad_out_weight])

    input_term = dot_to(grad_stack, qkv_flat, ((1,), (1,)))
    if shares == 2:
        mine = input_term.astype(low)
        away = lax.dynamic_slice_in_dim(mine, (1 - place) * share, share, 1)
        input_total = own_columns(mine).astype(single) + swap(away).astype(single)
    else:
        input_total = lax.psum_scatter(
            input_term.astype(low), "tensor", scatter_dimension=1, tiled=True
        ).astype(single)
    grad_tokens = (own_columns(grad_first) + input_total).astype(low)

    grad_rel_tables = sum(
        table_grads(
            [score_grads[group][page] for group in range(groups)], buckets[page : page + 1]
        )
        for page in range(pages)
    )
    normal_two = jnp.concatenate(normal_two_parts)

    def column_sum(matrix):
        return jnp.sum(matrix.astype(single), axis=0)

    smalls = [
        column_sum(grad_queries),
        column_sum(grad_values),
        own_columns(column_sum(grad_attended)),
        column_sum(grad_pre),
        own_columns(column_sum(grad_ffn)),
        own_columns(column_sum(grad_normed * normal_one)),
        own_columns(column_sum(grad_rows.astype(single) * normal_two)),
        own_columns(column_sum(grad_normed)),
        own_columns(column_sum(grad_rows)),
        grad_rel_tables.reshape(-1),
    ]
    packed = jnp.concatenate(smalls)
    packed = small_total(packed.reshape(-1, LANES)).reshape(-1)
    pieces = []
    at = 0
    for each in smalls:
        pieces.append(packed[at : at + each.shape[0]])
        at += each.shape[0]
    return (
        layer_out,
        grad_tokens,
        last_totals[0].astype(single).reshape(qkv_weight.shape),
        jnp.stack(pieces[0:2]),
        last_totals[1].astype(single),
        pieces[2],
        first_totals[1].astype(single),
        pieces[3],
        first_totals[0].astype(single),
        pieces[4],
        jnp.stack(pieces[5:7]),
        jnp.stack(pieces[7:9]),
        pieces[9].reshape(grad_rel_tables.shape),
    )


def solution(mesh):
    in_specs = (
        P("dp", None),
        P(None, None, "tensor"),
        P(None, "tensor"),
        P("tensor", None),
        P(),
        P(None, "tensor"),
        P("tensor"),
        P("tensor", None),
        P(),
        P(),
        P(),
        P(None, None, "tensor"),
        P("dp", None, None, None),
        P("dp", None),
        P("dp", "tensor"),
    )
    out_specs = (
        P("dp", "tensor"),
        P("dp", "tensor"),
        P(None, None, "tensor"),
        P(None, "tensor"),
        P("tensor", None),
        P("tensor"),
        P(None, "tensor"),
        P("tensor"),
        P("tensor", None),
        P("tensor"),
        P(None, "tensor"),
        P(None, "tensor"),
        P(None, None, "tensor"),
    )
    return jax.shard_map(body, mesh=mesh, in_specs=in_specs, out_specs=out_specs, check_vma=False)
```

```python
from functools import partial

import jax
import jax.numpy as jnp
from jax import lax
from jax.experimental import pallas as pl
from jax.experimental.pallas import tpu as pltpu
from jax.sharding import PartitionSpec as P

HEAD_DIM = 64


norm_epsilon = 1e-05
masked_score = -1e30


def exact_gelu(values):
    return jax.nn.gelu(values, approximate=False)


LANES = 128
STEP = 2048.0
RC = 576
RB = 96


def fwd_kernel(length, q_ref, k_ref, v_ref, b_ref, m_ref, t_ref, *refs):
    mixed_ref, p_ref, kz, vz, qz, tail, s_sc = refs[-7:]
    pair=pl.program_id(0)
    span=kz.shape[1]
    tall=qz.shape[0]
    full=length//LANES
    rest=length-full*LANES
    @pl.when(pair==0)
    def _():
        kz[...]=jnp.zeros_like(kz)
        vz[...]=jnp.zeros_like(vz)
        qz[...]=jnp.zeros_like(qz)
        tail[...]=jnp.zeros_like(tail)
        for t in range(3):
            tail[t,:length,:rest]=b_ref[0,t,:,full*LANES:]
    low=lax.broadcasted_iota(jnp.int32,(length,LANES),1)<HEAD_DIM
    kk=k_ref[...].astype(jnp.float32)*(HEAD_DIM**-0.5*STEP)
    vv=v_ref[...].astype(jnp.float32)
    kz[0,:length,:]=jnp.where(low,kk,0.0).astype(jnp.bfloat16)
    kz[1,:length,:]=jnp.where(low,0.0,kk).astype(jnp.bfloat16)
    vz[0,:length,:]=jnp.where(low,vv,0.0).astype(jnp.bfloat16)
    vz[1,:length,:]=jnp.where(low,0.0,vv).astype(jnp.bfloat16)
    qz[:length,:]=q_ref[...]
    valid=m_ref[...]>0
    for half in range(2):
        s_sc[half]=lax.dot_general(qz[...],kz[half],(((1,),(1,)),((),())),preferred_element_type=jnp.float32)
    for r in range(0,tall,RC):
        rc=min(RC,tall-r)
        bc=min(rc,length-r)
        tabs=[jnp.broadcast_to(t_ref[0,t:t+1,:],(bc,LANES)) for t in range(3)]
        parts=[[],[]]
        for c in range(span//LANES):
            code=None
            for t in range(3):
                idx=(b_ref[0,t,r:r+bc,c*LANES:(c+1)*LANES] if c<full else tail[t,r:r+bc,:])
                g=jnp.take_along_axis(tabs[t],idx,axis=1,mode="promise_in_bounds")
                code=g if code is None else code+g
            for half in range(2):
                bias=(code>>16 if half else code&0xFFFF).astype(jnp.float32)
                sc=s_sc[half,r:r+bc,c*LANES:(c+1)*LANES]+bias
                parts[half].append(jnp.where(valid[:,c*LANES:(c+1)*LANES],sc,masked_score))
        for half in range(2):
            ps=parts[half]
            m=ps[0]
            for x in ps[1:]: m=jnp.maximum(m,x)
            m=jnp.max(m,axis=1,keepdims=True)
            es=[jnp.exp((x-m)*(1.0/STEP)) for x in ps]
            tot=es[0]
            for x in es[1:]: tot=tot+x
            inv=1.0/jnp.sum(tot,axis=1,keepdims=True)
            pb=jnp.concatenate([x*inv for x in es],axis=1)
            if bc<rc:
                pb=jnp.concatenate([pb,jnp.zeros((rc-bc,span),jnp.float32)],axis=0)
            p_ref[half,r:r+rc,:]=pb.astype(jnp.bfloat16)
    acc=jnp.dot(p_ref[0],vz[0],preferred_element_type=jnp.float32)+jnp.dot(p_ref[1],vz[1],preferred_element_type=jnp.float32)
    mixed_ref[...]=acc[:length].astype(jnp.bfloat16)

def pack_tables(tables):
    fixed=jnp.round(jnp.transpose(tables,(2,0,1)).astype(jnp.float32)*STEP).astype(jnp.int32)
    return (fixed[1::2]<<16)+(fixed[0::2]+10240)

def attention_forward(q,k,v,buckets,mask_row,tables,at,heads,probs):
    length=q.shape[0]
    width=heads*HEAD_DIM
    packed=pack_tables(tables)
    own=pl.BlockSpec((length,LANES),lambda p:(0,p+at))
    span=-(-length//LANES)*LANES
    tall=-(-length//16)*16
    col=lambda p:(0,p)
    return pl.pallas_call(partial(fwd_kernel,length),
        grid=(heads//2,),
        in_specs=[own,
            own,
            own,
            pl.BlockSpec((1,3,length,length),lambda p:(0,0,0,0)),
            pl.BlockSpec((1,span),lambda p:(0,0)),
            pl.BlockSpec((1,3,LANES),lambda p:(p+at,0,0))]+([] if probs is None else [pl.BlockSpec(memory_space=pl.ANY)]),
        out_specs=[pl.BlockSpec((length,LANES),col),pl.BlockSpec((2,tall,span),lambda p:(p+at,0,0))],
        out_shape=[jax.ShapeDtypeStruct((length,width),jnp.bfloat16),jax.ShapeDtypeStruct((q.shape[1]//HEAD_DIM,tall,span),jnp.bfloat16)],
        input_output_aliases={} if probs is None else {6:1},
        scratch_shapes=[pltpu.VMEM((2,span,LANES),jnp.bfloat16),pltpu.VMEM((2,span,LANES),jnp.bfloat16),pltpu.VMEM((tall,LANES),jnp.bfloat16),pltpu.VMEM((3,tall,LANES),jnp.int32),pltpu.VMEM((2,tall,span),jnp.float32)],
        compiler_params=pltpu.CompilerParams(vmem_limit_bytes=48*1024*1024),
        name="attn_fwd",
    )(q,k,v,buckets,mask_row,packed,*([] if probs is None else [probs]))


def bwd_kernel(length, q_ref, k_ref, v_ref, dm_ref, p_ref, dq_ref, dk_ref, dv_ref, ds_ref, kz, vz, qz, dz, dp_sc):
    pair=pl.program_id(0)
    span=kz.shape[1]
    tall=qz.shape[0]
    @pl.when(pair==0)
    def _():
        kz[...]=jnp.zeros_like(kz)
        vz[...]=jnp.zeros_like(vz)
        qz[...]=jnp.zeros_like(qz)
        dz[...]=jnp.zeros_like(dz)
    low=lax.broadcasted_iota(jnp.int32,(length,LANES),1)<HEAD_DIM
    kk=k_ref[...].astype(jnp.float32)*HEAD_DIM**-0.5
    vv=v_ref[...].astype(jnp.float32)
    kz[0,:length,:]=jnp.where(low,kk,0.0).astype(jnp.bfloat16)
    kz[1,:length,:]=jnp.where(low,0.0,kk).astype(jnp.bfloat16)
    vz[0,:length,:]=jnp.where(low,vv,0.0).astype(jnp.bfloat16)
    vz[1,:length,:]=jnp.where(low,0.0,vv).astype(jnp.bfloat16)
    qz[:length,:]=(q_ref[...].astype(jnp.float32)*HEAD_DIM**-0.5).astype(jnp.bfloat16)
    dz[:length,:]=dm_ref[...]
    for half in range(2):
        dp_sc[half]=lax.dot_general(dz[...],vz[half],(((1,),(1,)),((),())),preferred_element_type=jnp.float32)
    for half in range(2):
        for r in range(0,tall,RB):
            rc=min(RB,tall-r)
            p=p_ref[half,r:r+rc,:].astype(jnp.float32)
            dp=dp_sc[half,r:r+rc,:]
            delta=jnp.sum(p*dp,axis=1,keepdims=True)
            ds_ref[half,r:r+rc,:]=(p*(dp-delta)).astype(jnp.bfloat16)
    dq=jnp.dot(ds_ref[0],kz[0],preferred_element_type=jnp.float32)+jnp.dot(ds_ref[1],kz[1],preferred_element_type=jnp.float32)
    dq_ref[...]=dq[:length].astype(jnp.bfloat16)
    turned=(((0,),(0,)),((),()))
    grad=lambda left,right: lax.dot_general(left,right,turned,preferred_element_type=jnp.float32)[:length]
    dk_ref[...]=jnp.where(low,grad(ds_ref[0],qz[...]),grad(ds_ref[1],qz[...])).astype(jnp.bfloat16)
    dv_ref[...]=jnp.where(low,grad(p_ref[0],dz[...]),grad(p_ref[1],dz[...])).astype(jnp.bfloat16)

def attention_backward(q,k,v,dm,probs):
    length=q.shape[0]
    heads,tall,span=probs.shape
    width=heads*HEAD_DIM
    col=pl.BlockSpec((length,LANES),lambda p:(0,p))
    big=pl.BlockSpec((2,tall,span),lambda p:(p,0,0))
    flat=jax.ShapeDtypeStruct((length,width),jnp.bfloat16)
    return pl.pallas_call(partial(bwd_kernel,length),
        grid=(heads//2,),
        in_specs=[col,col,col,col,big],
        out_specs=[col,col,col,big],
        out_shape=[flat,flat,flat,jax.ShapeDtypeStruct(probs.shape,jnp.bfloat16)],
        scratch_shapes=[pltpu.VMEM((2,span,LANES),jnp.bfloat16),pltpu.VMEM((2,span,LANES),jnp.bfloat16),pltpu.VMEM((tall,LANES),jnp.bfloat16),pltpu.VMEM((tall,LANES),jnp.bfloat16),pltpu.VMEM((2,tall,span),jnp.float32)],
        compiler_params=pltpu.CompilerParams(vmem_limit_bytes=48*1024*1024),
        name="attn_bwd",
    )(q,k,v,dm,probs)

TQ=32
GROUP=2
HIGH=4
def table_kernel(length, count, *refs):
    ds_refs,(b_ref,o_ref,dt,tail,acc)=refs[:count],refs[count:]
    step=pl.program_id(0)
    span=ds_refs[0].shape[2]
    heads=sum(ref.shape[0] for ref in ds_refs)
    full=length//LANES
    rest=length-full*LANES
    low_count=LANES//HIGH
    @pl.when(step==0)
    def _():
        acc[...]=jnp.zeros_like(acc)
        tail[...]=jnp.zeros_like(tail)
        if heads<8:
            dt[...]=jnp.zeros_like(dt)
    for t in range(3):
        tail[t,:,:rest]=b_ref[0,t,:,full*LANES:]
    h=0
    for ref in ds_refs:
        for inner in range(ref.shape[0]):
            for c in range(span//LANES):
                dt[c,pl.ds(h,TQ,8),:]=ref[inner,:,c*LANES:(c+1)*LANES].astype(jnp.float32)
            h+=1
    ladder=lax.broadcasted_iota(jnp.int32,(8,LANES),0)
    for i0 in range(0,TQ,GROUP):
        lefts=[[] for _ in range(3*HIGH)]
        rights=[[] for _ in range(3*low_count//8)]
        for i in range(i0,i0+GROUP):
            for c in range(span//LANES):
                d8=dt[c,i*8:(i+1)*8,:]
                for t in range(3):
                    row=b_ref[0,t,i:i+1,c*LANES:(c+1)*LANES] if c<full else tail[t,i:i+1,:]
                    row=jnp.broadcast_to(row,(8,LANES))
                    high=lax.shift_right_logical(row,low_count.bit_length()-1)
                    low=(row&(low_count-1))-ladder
                    for m in range(HIGH):
                        lefts[t*HIGH+m].append(jnp.where(high==m,d8,0.0))
                    for m in range(low_count//8):
                        rights[t*(low_count//8)+m].append(jnp.where(low==8*m,1.0,0.0))
        left=jnp.concatenate([jnp.concatenate(x,axis=1) for x in lefts],axis=0).astype(jnp.bfloat16)
        right=jnp.concatenate([jnp.concatenate(x,axis=1) for x in rights],axis=0).astype(jnp.bfloat16)
        acc[...]+=lax.dot_general(left,right,(((1,),(1,)),((),())),preferred_element_type=jnp.float32)
    o_ref[...]=acc[...]

def table_grads(ds,buckets):
    heads=sum(each.shape[0] for each in ds)
    _,tall,span=ds[0].shape
    length=buckets.shape[2]
    low_count=LANES//HIGH
    out=pl.pallas_call(partial(table_kernel,length,len(ds)),
        grid=(-(-tall//TQ),),
        in_specs=[pl.BlockSpec((each.shape[0],TQ,span),lambda i:(0,i,0)) for each in ds]+[pl.BlockSpec((1,3,TQ,length),lambda i:(0,0,i,0))],
        out_specs=pl.BlockSpec((24*HIGH,3*low_count),lambda i:(0,0)),
        out_shape=jax.ShapeDtypeStruct((24*HIGH,3*low_count),jnp.float32),
        scratch_shapes=[pltpu.VMEM((span//LANES,TQ*8,LANES),jnp.float32),pltpu.VMEM((3,TQ,LANES),jnp.int32),pltpu.VMEM((24*HIGH,3*low_count),jnp.float32)],
        compiler_params=pltpu.CompilerParams(vmem_limit_bytes=48*1024*1024),
        name="table_grads",
    )(*ds,buckets)
    own=jnp.stack([out[t*8*HIGH:(t+1)*8*HIGH,t*low_count:(t+1)*low_count] for t in range(3)])
    own=own.reshape(3,HIGH,8,low_count)[:,:,:heads]
    return jnp.transpose(own,(0,1,3,2)).reshape(3,LANES,heads)


def rows_cut(length):
    first = -(-length // 32) * 16
    return ((0, first), (first, length)) if first < length else ((0, length),)


def norm_forward(values, gain, shift):
    width = values.shape[1]
    center = jnp.sum(values, axis=-1, keepdims=True) / width
    deviation = values - center
    spread = jnp.sum(deviation * deviation, axis=-1, keepdims=True) / width
    scaling = lax.rsqrt(spread + norm_epsilon)
    normal = deviation * scaling
    return normal * gain + shift, normal, scaling


def norm_backward(grad_out, normal, scaling, gain):
    width = grad_out.shape[1]
    scaled = grad_out * gain
    first = jnp.sum(scaled, axis=-1, keepdims=True) / width
    second = jnp.sum(scaled * normal, axis=-1, keepdims=True) / width
    return scaling * (scaled - first - normal * second)


def dot_to(left, right, dims=((1,), (0,))):
    return lax.dot_general(left, right, (dims, ((), ())), preferred_element_type=jnp.float32)


def dp_bit(over):
    return lax.axis_index("dp") // over % 2


CORE, OVER_Y = 1, 2


def move(matrix, partner, senders=range(4)):
    return lax.ppermute(matrix, "dp", [(i, partner(i)) for i in range(16) if i // 4 in senders])


def swap(matrix):
    return lax.ppermute(matrix, "tensor", [(0, 1), (1, 0)])


def over_core(i):
    return i ^ CORE


def over_y(i):
    return i ^ OVER_Y


def outer_z(i):
    return i ^ 4


def inner_z(i):
    return i ^ 12


def added(left, right):
    return (left.astype(jnp.float32) + right.astype(jnp.float32)).astype(jnp.bfloat16)


EVERY = range(4)


def total_steps(own, away):
    z = lax.axis_index("dp") // 4
    (other,) = yield ((away, move, over_y, EVERY),)
    own = added(own, other)
    (other,) = yield ((own, move, outer_z, (0, 3)),)
    own = added(own, other)
    (other,) = yield ((own, move, inner_z, (1, 2)),)
    own = added(own, other)
    (other,) = yield ((own, move, outer_z, (1, 2)),)
    own = jnp.where((z == 0) | (z == 3), other, own)
    (other,) = yield ((own, move, over_y, EVERY),)
    third, fourth = yield (own, move, over_core, EVERY), (other, move, over_core, EVERY)
    return own, other, third, fourth


def doubling_steps(matrix):
    for partner in (over_core, over_y, outer_z, inner_z):
        (other,) = yield ((matrix, move, partner, EVERY),)
        matrix = matrix + other
    return matrix


def swap_step(matrix):
    (other,) = yield ((matrix, swap),)
    return other


class Relay:
    def __init__(self):
        self.running = {}
        self.done = {}

    def begin(self, name, chain):
        self.running[name] = (chain, next(chain))

    def step(self, names, tied=()):
        sent = tuple(tuple(each[0] for each in self.running[name][1]) for name in names)
        sent, tied = lax.optimization_barrier((sent, tied))
        moved = tuple(
            tuple(ask[1](matrix, *ask[2:]) for matrix, ask in zip(group, self.running[name][1]))
            for name, group in zip(names, sent)
        )
        moved = lax.optimization_barrier(moved)
        for name, others in zip(names, moved):
            chain = self.running[name][0]
            try:
                self.running[name] = (chain, chain.send(others))
            except StopIteration as stop:
                self.done[name] = stop.value
                del self.running[name]
        return tied


def late_kernel(count, first, order_ref, tokens_ref, *refs):
    matrix = (pl.program_id(0) // 2 + first) ^ order_ref[0]
    *grads, attended_ref, out_ref = refs
    turned = (((0,), (0,)), ((), ()))

    def product(left, right):
        return lax.dot_general(left, right, turned, preferred_element_type=jnp.float32)

    for which in range(3):

        @pl.when(matrix == which)
        def _():
            out_ref[...] = product(tokens_ref[...], grads[which][...]).astype(jnp.bfloat16)

    @pl.when(matrix == 3)
    def _():
        rows = out_ref.shape[0] // count
        for part in range(count):
            out_ref[part * rows : (part + 1) * rows, :] = product(
                grads[3 + part][...], attended_ref[...]
            ).astype(jnp.bfloat16)


def late_grads(order, first, tokens, grads, mixed_groups, grad_attended):
    count = len(mixed_groups)
    length, width = tokens.shape
    rows = width // 2
    wide = grad_attended.shape[1] // 2
    whole = [pl.BlockSpec(each.shape, lambda i, order: (0, 0)) for each in (*grads, *mixed_groups)]
    return pl.pallas_call(
        partial(late_kernel, count, first),
        grid_spec=pltpu.PrefetchScalarGridSpec(
            num_scalar_prefetch=1,
            grid=(4,),
            in_specs=[
                pl.BlockSpec((length, rows), lambda i, order: (0, i % 2)),
                *whole,
                pl.BlockSpec((length, wide), lambda i, order: (0, i % 2)),
            ],
            out_specs=pl.BlockSpec((rows, wide), lambda i, order: (i, 0)),
        ),
        out_shape=jax.ShapeDtypeStruct((4 * rows, wide), jnp.bfloat16),
        compiler_params=pltpu.CompilerParams(vmem_limit_bytes=58 * 1024 * 1024),
        name="late_grads",
    )(order, tokens, *grads, *mixed_groups, grad_attended)


def early_kernel(hidden_refs, ffn_refs, normed_ref, pre_refs, out_ref):
    turned = (((0,), (0,)), ((), ()))
    cut = ffn_refs[0].shape[0]

    def product(left, right):
        return lax.dot_general(left, right, turned, preferred_element_type=jnp.float32)

    @pl.when(pl.program_id(0) < 4)
    def _():
        total = sum(product(left[...], right[...]) for left, right in zip(hidden_refs, ffn_refs))
        out_ref[...] = total.astype(jnp.bfloat16)

    @pl.when(pl.program_id(0) >= 4)
    def _():
        total = product(normed_ref[:cut, :], pre_refs[0][...])
        out_ref[...] = (total + product(normed_ref[cut:, :], pre_refs[1][...])).astype(jnp.bfloat16)


def early_grads(hidden, grad_ffn, normed_low, grad_pre):
    length, width = normed_low.shape
    rows = width // 2

    def specs(parts, columns, index):
        return [pl.BlockSpec((part.shape[0], columns), index) for part in parts]

    return pl.pallas_call(
        early_kernel,
        grid=(8,),
        in_specs=[
            specs(hidden, rows, lambda i: (0, jnp.minimum(i, 3))),
            specs(grad_ffn, width, lambda i: (0, 0)),
            pl.BlockSpec((length, rows), lambda i: (0, jnp.where(i < 4, 0, i % 2))),
            specs(grad_pre, width, lambda i: (0, jnp.where(i < 6, 0, 1))),
        ],
        out_specs=pl.BlockSpec((rows, width), lambda i: (i, 0)),
        out_shape=jax.ShapeDtypeStruct((8 * rows, width), jnp.bfloat16),
        compiler_params=pltpu.CompilerParams(vmem_limit_bytes=58 * 1024 * 1024),
        name="early_grads",
    )(hidden, grad_ffn, normed_low, grad_pre)


def place_kernel(count, order_ref, *refs):
    *parts, qkv_ref, out_ref = refs
    step = pl.program_id(0)
    place = step ^ order_ref[0]
    rows = parts[0].shape[0]
    for which in range(4):

        @pl.when((place == which) & (step < 3))
        def _():
            for at in range(count):
                qkv_ref[at * rows : (at + 1) * rows, :] = parts[which * count + at][...].astype(
                    jnp.float32
                )

        @pl.when((place == which) & (step == 3))
        def _():
            wide = qkv_ref.shape[1]
            for at in range(count):
                out_ref[:, at * wide : (at + 1) * wide] = parts[which * count + at][...].astype(
                    jnp.float32
                )


def placed(order, parts):
    count = len(parts[0])
    flat = [each for group in parts for each in group]
    rows, wide = flat[0].shape
    return pl.pallas_call(
        partial(place_kernel, count),
        grid_spec=pltpu.PrefetchScalarGridSpec(
            num_scalar_prefetch=1,
            grid=(4,),
            in_specs=[pl.BlockSpec((rows, wide), lambda i, order: (0, 0)) for _ in flat],
            out_specs=[
                pl.BlockSpec((count * rows, wide), lambda i, order: (jnp.minimum(i, 2), 0)),
                pl.BlockSpec((rows, count * wide), lambda i, order: (0, 0)),
            ],
        ),
        out_shape=[
            jax.ShapeDtypeStruct((3 * count * rows, wide), jnp.float32),
            jax.ShapeDtypeStruct((rows, count * wide), jnp.float32),
        ],
        compiler_params=pltpu.CompilerParams(vmem_limit_bytes=48 * 1024 * 1024),
        name="placed",
    )(order, *flat)


def sums_kernel(place_ref, dq, dv, attended, pre, ffn, normed, one, rows, two, out_ref):
    single = jnp.float32
    cut = two[0].shape[0]

    def total(terms):
        return sum(jnp.sum(term, axis=0, keepdims=True) for term in terms)

    at = 0
    for terms in (
        [dq[...].astype(single)],
        [dv[...].astype(single)],
        [attended[...].astype(single)],
        [part[...].astype(single) for part in pre],
        [part[...].astype(single) for part in ffn],
        [normed[...] * one[...]],
        [
            rows[:cut, :].astype(single) * two[0][...],
            rows[cut:, :].astype(single) * two[1][...],
        ],
        [normed[...]],
        [rows[...].astype(single)],
    ):
        row = total(terms)
        out_ref[:, at : at + row.shape[1]] = row
        at += row.shape[1]


def column_sums(place, dq, dv, attended, pre, ffn, normed, one, rows, two):
    share = rows.shape[1]

    def whole(each):
        return pl.BlockSpec(each.shape, lambda i, place: (0, 0))

    def own(each):
        return pl.BlockSpec((each.shape[0], share), lambda i, place: (0, place[0]))

    arrays = (dq, dv, attended, pre, ffn, normed, one, rows, two)
    kinds = (whole, whole, own, whole, own, own, own, whole, own)
    widths = [dq.shape[1], dv.shape[1], share, pre[0].shape[1]] + [share] * 5
    return pl.pallas_call(
        sums_kernel,
        grid_spec=pltpu.PrefetchScalarGridSpec(
            num_scalar_prefetch=1,
            grid=(1,),
            in_specs=[
                [kind(part) for part in each] if isinstance(each, (list, tuple)) else kind(each)
                for kind, each in zip(kinds, arrays)
            ],
            out_specs=pl.BlockSpec((1, sum(widths)), lambda i, place: (0, 0)),
        ),
        out_shape=jax.ShapeDtypeStruct((1, sum(widths)), jnp.float32),
        compiler_params=pltpu.CompilerParams(vmem_limit_bytes=48 * 1024 * 1024),
        name="column_sums",
    )(place.reshape(1), *arrays), widths


def body(
    tokens,
    qkv_weight,
    qv_bias,
    out_weight,
    out_bias,
    up_weight,
    up_bias,
    down_weight,
    down_bias,
    norm_gain,
    norm_shift,
    rel_tables,
    buckets,
    key_mask,
    cotangent,
):
    single = jnp.float32
    low = jnp.bfloat16
    shares = lax.axis_size("tensor")
    place = lax.axis_index("tensor")
    width = tokens.shape[1]
    share = width // shares
    pages, _, length, _ = buckets.shape
    local_width = qkv_weight.shape[2]

    def own_columns(matrix):
        return lax.dynamic_slice_in_dim(matrix, place * share, share, matrix.ndim - 1)

    def summed(terms):
        return sum(each.astype(single) for each in terms)

    def branch_total(summand):
        mine = summand.astype(low)
        if shares == 2:
            return mine, swap(mine)
        return (lax.psum(mine, "tensor"),)

    if shares == 2:
        if lax.axis_size("dp") == 16:
            count = out_weight.shape[0] // 2
            core = dp_bit(CORE)
            one = swap(lax.dynamic_slice_in_dim(out_weight, core * count, count, 0))
            two = move(one, over_core)
            out_all = jnp.concatenate(
                [out_weight, jnp.where(core == 0, one, two), jnp.where(core == 0, two, one)]
            )
        else:
            out_all = jnp.concatenate([out_weight, swap(out_weight)], axis=0)
        other = swap(cotangent)
        grad_rows = jnp.where(
            place == 0,
            jnp.concatenate([cotangent, other], axis=1),
            jnp.concatenate([other, cotangent], axis=1),
        )
    qkv_parts = jnp.transpose(qkv_weight, (1, 0, 2))
    queries = (dot_to(tokens, qkv_parts[0]) + qv_bias[0].astype(single)).astype(low)
    keys_all = dot_to(tokens, qkv_parts[1]).astype(low)
    values_all = (dot_to(tokens, qkv_parts[2]) + qv_bias[1].astype(single)).astype(low)

    span = -(-length // LANES) * LANES
    mask_rows = jnp.pad(key_mask, ((0, 0), (0, span - length)))
    pairs = local_width // LANES
    groups = 2 if pairs % 2 == 0 else 1
    group_width = local_width // groups
    mixed_groups = []
    probs = [None] * pages
    for group in range(groups):
        parts = []
        for page in range(pages):
            part, probs[page] = attention_forward(
                queries[page * length : (page + 1) * length],
                keys_all[page * length : (page + 1) * length],
                values_all[page * length : (page + 1) * length],
                buckets[page : page + 1],
                mask_rows[page : page + 1],
                rel_tables,
                group * group_width // LANES,
                group_width // HEAD_DIM,
                probs[page],
            )
            parts.append(part)
        mixed_groups.append(jnp.concatenate(parts))
    mixed = jnp.concatenate(mixed_groups, axis=1)
    if shares == 2:
        mixed_all = jnp.concatenate(mixed_groups + [swap(each) for each in mixed_groups], axis=1)
        attended = dot_to(mixed_all, out_all)
    else:
        attended = summed(branch_total(dot_to(mixed, out_weight)))
        grad_rows = lax.all_gather(cotangent, "tensor", axis=1, tiled=True)

    gains = norm_gain.astype(single)
    shifts = norm_shift.astype(single)
    first = tokens.astype(single) + (attended + out_bias.astype(single))
    normed, normal_one, scaling_one = norm_forward(first, gains[0], shifts[0])
    normed_low = normed.astype(low)

    cuts = rows_cut(tokens.shape[0])
    slopes = []
    hidden_parts = []
    totals = []
    for start, stop in cuts:
        pre_act = dot_to(normed_low[start:stop], up_weight) + up_bias.astype(single)
        hidden, gelu_pull = jax.vjp(exact_gelu, pre_act)
        hidden_parts.append(hidden.astype(low))
        slopes.append(gelu_pull)
        partial_sum = dot_to(hidden_parts[-1], down_weight).astype(low)
        normed_low, partial_sum = lax.optimization_barrier((normed_low, partial_sum))
        totals.append(branch_total(partial_sum))
    outs = []
    grad_ffn_parts = []
    grad_pre_parts = []
    grad_second_parts = []
    normal_two_parts = []
    branch = []
    for at, (start, stop) in enumerate(cuts):
        if at:
            total, branch[-1] = lax.optimization_barrier((totals[at], branch[-1]))
        else:
            total = totals[at]
        second = normed[start:stop] + (summed(total) + down_bias.astype(single))
        result, normal_two, scaling_two = norm_forward(second, gains[1], shifts[1])
        outs.append(own_columns(result.astype(low)))
        normal_two_parts.append(normal_two)
        grad_second = norm_backward(
            grad_rows[start:stop].astype(single), normal_two, scaling_two, gains[1]
        )
        grad_second_parts.append(grad_second)
        grad_ffn = grad_second.astype(low)
        grad_ffn_parts.append(grad_ffn)
        grad_hidden = dot_to(grad_ffn, down_weight, ((1,), (1,)))
        grad_pre = slopes[at](grad_hidden)[0].astype(low)
        grad_pre_parts.append(grad_pre)
        if start == 0:
            branch.append(dot_to(grad_pre, up_weight, ((1,), (1,))).astype(low))
    layer_out = jnp.concatenate(outs)
    grad_ffn = jnp.concatenate(grad_ffn_parts)
    grad_pre = jnp.concatenate(grad_pre_parts)
    hidden_low = jnp.concatenate(hidden_parts)
    over_rows = ((0,), (0,))
    by_hand = (
        lax.axis_size("dp") == 16
        and shares == 2
        and groups == 2
        and pages == 1
        and hidden_low.shape[1] == 2 * width
        and len(cuts) == 2
    )
    if by_hand:
        early = early_grads(hidden_parts, grad_ffn_parts, normed_low, grad_pre_parts)
        branch[0] = branch_total(branch[0])
        early, grad_pre_last, branch[0] = lax.optimization_barrier(
            (early, grad_pre_parts[-1], branch[0])
        )
        early = lax.psum_scatter(early, "dp", scatter_dimension=0, tiled=True)
        branch.append(dot_to(grad_pre_last, up_weight, ((1,), (1,))))
        branch[-1], normal_two_parts, grad_second_parts = lax.optimization_barrier(
            (branch[-1].astype(low), normal_two_parts, grad_second_parts)
        )
    else:
        grad_down_weight = dot_to(hidden_low, grad_ffn, over_rows).astype(low)
        grad_up_weight = dot_to(normed_low, grad_pre, over_rows).astype(low)
        down_total, up_total = lax.psum((grad_down_weight, grad_up_weight), "dp")
        if len(cuts) > 1:
            grad_pre_last = grad_pre_parts[-1]
            branch.append(dot_to(grad_pre_last, up_weight, ((1,), (1,))).astype(low))
    branch = [
        summed(each if isinstance(each, tuple) else branch_total(each)) for each in branch
    ]

    grad_normed = jnp.concatenate(
        [part + more for part, more in zip(grad_second_parts, branch)]
    )
    grad_first = norm_backward(grad_normed, normal_one, scaling_one, gains[0])
    grad_attended = grad_first.astype(low)
    grad_mixed = dot_to(grad_attended, out_weight, ((1,), (1,))).astype(low)

    backward = [
        attention_backward(
            queries[page * length : (page + 1) * length],
            keys_all[page * length : (page + 1) * length],
            values_all[page * length : (page + 1) * length],
            grad_mixed[page * length : (page + 1) * length],
            probs[page],
        )
        for page in range(pages)
    ]
    grad_queries, grad_keys, grad_values = (
        jnp.concatenate([each[at] for each in backward]) for at in range(3)
    )
    score_grads = [each[3] for each in backward]

    def sums():
        return column_sums(
            place,
            grad_queries,
            grad_values,
            grad_attended,
            list(grad_pre_parts),
            list(grad_ffn_parts),
            grad_normed,
            normal_one,
            cotangent,
            list(normal_two_parts),
        )

    def all_tables(score_grads):
        return sum(
            table_grads([score_grads[page]], buckets[page : page + 1]) for page in range(pages)
        )

    if by_hand:
        order = (dp_bit(OVER_Y) + 2 * dp_bit(CORE)).astype(jnp.int32).reshape(1)
        late_inputs = (
            tokens,
            (grad_queries, grad_keys, grad_values),
            mixed_groups,
            grad_attended,
        )
        away, late_inputs = lax.optimization_barrier(
            (late_grads(order, 2, *late_inputs), late_inputs)
        )
        late = added(late_grads(order, 0, *late_inputs), move(away, over_core))
        relay = Relay()
        count = width // 2
        for at in range(2):
            own = slice(at * count, (at + 1) * count)
            away = slice(width + at * count, width + (at + 1) * count)
            relay.begin(at, total_steps(late[own], late[away]))
        grad_queries, grad_keys, grad_values = relay.step(
            [0], (grad_queries, grad_keys, grad_values)
        )
        input_term = sum(
            dot_to(each, qkv_parts[at], ((1,), (1,)))
            for at, each in enumerate((grad_queries, grad_keys, grad_values))
        ).astype(low)
        packed, widths = sums()
        relay.begin(
            "tokens",
            swap_step(lax.dynamic_slice_in_dim(input_term, (1 - place) * share, share, 1)),
        )
        (score_grads,) = relay.step([0, 1, "tokens"], (score_grads,))
        grad_rel_tables = all_tables(score_grads)
        packed = jnp.concatenate(
            [packed.reshape(-1, LANES), grad_rel_tables.reshape(-1, LANES)]
        )
        relay.begin("small", doubling_steps(packed))
        (early,) = relay.step([0, 1, "small"], (early,))
        early = lax.all_gather(early, "dp", axis=0, tiled=True)
        input_total = own_columns(input_term).astype(single) + relay.done["tokens"].astype(single)
        for names in ([0, 1, "small"], [0, 1, "small"], [0, 1, "small"]):
            relay.step(names)
        (early,) = relay.step([1], (early,))
        packed = relay.done["small"]
        parts = list(zip(relay.done[0], relay.done[1]))
        qkv_total, out_total = placed(order, parts)
        down_total = early[: 2 * width]
        up_total = jnp.concatenate([early[2 * width : 3 * width], early[3 * width :]], axis=1)
        qkv_total = qkv_total.reshape(3, width, local_width)
    else:
        grad_qkv_weight = [
            dot_to(tokens, each, over_rows).astype(low)
            for each in (grad_queries, grad_keys, grad_values)
        ]
        grad_out_weight = dot_to(mixed, grad_attended, over_rows).astype(low)
        *qkv_total, out_total = lax.psum((*grad_qkv_weight, grad_out_weight), "dp")
        qkv_total = jnp.stack(qkv_total).astype(single)
        out_total = out_total.astype(single)
    if not by_hand:
        input_term = sum(
            dot_to(each, qkv_parts[at], ((1,), (1,)))
            for at, each in enumerate((grad_queries, grad_keys, grad_values))
        )
        input_total = lax.psum_scatter(
            input_term.astype(low), "tensor", scatter_dimension=1, tiled=True
        ).astype(single)
        packed, widths = sums()
        grad_rel_tables = all_tables(score_grads)
        packed = lax.psum(
            jnp.concatenate([packed.reshape(-1, LANES), grad_rel_tables.reshape(-1, LANES)]), "dp"
        )
    grad_tokens = (own_columns(grad_first) + input_total).astype(low)

    packed = packed.reshape(-1)
    pieces = []
    at = 0
    for each in widths:
        pieces.append(packed[at : at + each])
        at += each
    grad_rel_tables = packed[at:].reshape(grad_rel_tables.shape)
    return (
        layer_out,
        grad_tokens,
        jnp.transpose(qkv_total, (1, 0, 2)),
        jnp.stack(pieces[0:2]),
        out_total,
        pieces[2],
        up_total.astype(single),
        pieces[3],
        down_total.astype(single),
        pieces[4],
        jnp.stack(pieces[5:7]),
        jnp.stack(pieces[7:9]),
        grad_rel_tables,
    )


def solution(mesh):
    in_specs = (
        P("dp", None),
        P(None, None, "tensor"),
        P(None, "tensor"),
        P("tensor", None),
        P(),
        P(None, "tensor"),
        P("tensor"),
        P("tensor", None),
        P(),
        P(),
        P(),
        P(None, None, "tensor"),
        P("dp", None, None, None),
        P("dp", None),
        P("dp", "tensor"),
    )
    out_specs = (
        P("dp", "tensor"),
        P("dp", "tensor"),
        P(None, None, "tensor"),
        P(None, "tensor"),
        P("tensor", None),
        P("tensor"),
        P(None, "tensor"),
        P("tensor"),
        P("tensor", None),
        P("tensor"),
        P(None, "tensor"),
        P(None, "tensor"),
        P(None, None, "tensor"),
    )
    return jax.shard_map(body, mesh=mesh, in_specs=in_specs, out_specs=out_specs, check_vma=False)
```
